32 devices in a mesh: section: 2 (over x), ctx: 16 (over z, y, core).
Axes of the slice: x: 2, y: 2, z: 4, core: 2. Of those that a mesh axis runs over, the one named last changes fastest.
Arguments:
- earlier_span: bfloat16 [2, 2048, 4096], P('section', 'ctx'), may hold values from -6 to 6
- span_inputs: bfloat16 [2, 2048, 4096], P('section', 'ctx'), may hold values from -24 to 24
- next_inputs: bfloat16 [2048, 4096], P('ctx'), may hold values from -24 to 24
- block_list: int32 [16, 4], replicated, may hold values from -1 to 31, as said below
- q_gain: float32 [2, 4096], P('section'), may hold values from 0.5 to 8
- k_gain: float32 [2, 4096], P('section'), may hold values from -8 to 8
- out_gain: float32 [2, 4096], P('section'), may hold values from 0.5 to 2
Outputs:
- second_out: bfloat16 [2, 2048, 4096], P('section', 'ctx')
The draws below stay inside these ranges and needn't reach their ends.
Inputs may be any that keep to these rules, and one draw needn't show every extreme that they name: `block_list`: row i names key block 16 + i, then 16 + i - 1, then 1 increasing blocks r from 0 to 13, the same in every row, then the blocks 16 + r in the same order, each replaced by -1 unless it is at least 2 blocks before 16 + i. The last row has no -1.
All inputs are finite; a program needn't handle non-finite values.
Results may differ from the reference program's by a relative error of at most 0.0055.
The reference program's roundings to bfloat16 on the way count: a program that leaves them out, or rounds other values in their place, can miss the bound.
Values may be sent and summed in bfloat16 or wider, within the bound.
A program may use at most 64 MiB of HBM per device.

```python
import math
import jax
import jax.numpy as jnp
from jax import lax

HEADS = 32
HD = 128
BLOCK = 128
LOCAL = 2
NR = 1
WIDTH = 4096
NQ = 16
SPAN = 2048
NSEL = 4
SECTIONS = 2


def gain_signs(key):
    flips = jax.random.randint(jax.random.fold_in(key, 11), (SECTIONS, WIDTH), 0, 2)
    return (2 * flips - 1).astype(jnp.float32)


def gain_sizes(key):
    bottom, top = (0.5, 2.0)
    return jnp.exp(jax.random.uniform(key, (SECTIONS, WIDTH), jnp.float32, math.log(bottom), math.log(top)))


def draw_q_gain(key, part):
    return gain_sizes(jax.random.fold_in(key, 21))


def draw_k_gain(key, part):
    return gain_signs(key) * gain_sizes(jax.random.fold_in(key, 22))


def draw_rows_common(key, shape):
    return jnp.clip(jax.random.normal(key, shape, jnp.float32), -6.0, 6.0)


def draw_span_inputs(key, part):
    return draw_rows_common(jax.random.fold_in(key, 31), (SECTIONS, SPAN, WIDTH)).astype(jnp.bfloat16)


def draw_next_inputs(key, part):
    return draw_rows_common(jax.random.fold_in(key, 32), (SPAN, WIDTH)).astype(jnp.bfloat16)


def draw_block_list(key, part):
    order = jax.random.permutation(jax.random.fold_in(key, 41), NQ - LOCAL)
    offsets = jnp.sort(order[:NR]).astype(jnp.int32)
    query_block = jnp.arange(NQ, dtype=jnp.int32)
    global_block = NQ + query_block
    own = global_block[:, None]
    before = (global_block - 1)[:, None]
    earlier = jnp.broadcast_to(offsets[None, :], (NQ, NR))
    later = offsets[None, :] + NQ
    later = jnp.where(later <= global_block[:, None] - LOCAL, later, -1)
    return jnp.concatenate([own, before, earlier, later], axis=1).astype(jnp.int32)


def block_levels(stream_key, shape, cuts, smallest, largest):
    loudness = 1.0
    for axis_at, shards_of in cuts:
        draws = jax.random.uniform(jax.random.fold_in(jax.random.fold_in(stream_key, 6), axis_at), (shards_of,), jnp.float32, smallest / len(cuts), largest / len(cuts))
        loudness = loudness * jnp.repeat(jnp.exp(draws), shape[axis_at] // shards_of).reshape((-1,) + (1,) * (len(shape) - 1 - axis_at))
    return loudness


def gaussian(rng, dims, spread, limit, split=(), held_as=jnp.bfloat16):
    drawn = jax.random.normal(rng, dims, jnp.float32) * spread
    if len(split) > 0:
        drawn = block_levels(rng, dims, split, -0.22, 0.18) * drawn
    return jnp.clip(drawn, min=-limit, max=limit).astype(held_as)


def setup_inputs(seed: int = 0) -> dict:
    seeds = jax.random.split(jax.random.key(seed), 8)
    earlier_span = gaussian(seeds[0], (SECTIONS, SPAN, WIDTH), 1.0, 6.0, ((0, 2), (1, 16)))
    span_inputs = draw_span_inputs(jax.random.fold_in(seeds[7], 71), 0)
    next_inputs = draw_next_inputs(jax.random.fold_in(seeds[7], 71), 0)
    block_list = draw_block_list(jax.random.fold_in(seeds[7], 71), 0)
    q_gain = draw_q_gain(jax.random.fold_in(seeds[7], 71), 0)
    k_gain = draw_k_gain(jax.random.fold_in(seeds[7], 71), 0)
    out_gain = jnp.clip(jnp.exp(math.log(2.0) - 1.3862944 * jax.random.uniform(seeds[6], (SECTIONS, WIDTH), jnp.float32) ** block_levels(seeds[6], (SECTIONS, WIDTH), ((0, 2),), -0.2, 0.2)), 0.5, 2.0)
    return dict(earlier_span=earlier_span, span_inputs=span_inputs, next_inputs=next_inputs, block_list=block_list, q_gain=q_gain, k_gain=k_gain, out_gain=out_gain)


def normalize(rows):
    widened = rows.astype(jnp.float32).reshape(rows.shape[0], HEADS, HD)
    return widened * lax.rsqrt(lax.optimization_barrier(jnp.mean(widened * widened, axis=-1, keepdims=True)) + 1e-06)

def attend_block(query_rows, key_rows, entries, global_block, gain_query, gain_key, gain_out):
    key_flat = key_rows.reshape(NSEL * BLOCK, WIDTH)
    queries = (normalize(query_rows) * gain_query.reshape(HEADS, HD) * HD ** (-0.5)).astype(jnp.bfloat16)
    keys = (normalize(key_flat) * gain_key.reshape(HEADS, HD)).astype(jnp.bfloat16)
    values = key_flat.reshape(NSEL * BLOCK, HEADS, HD)
    key_entry = jnp.repeat(entries, BLOCK)
    key_pos = jnp.arange(NSEL * BLOCK, dtype=jnp.int32) % BLOCK
    query_pos = jnp.arange(BLOCK, dtype=jnp.int32)
    allowed = (key_entry >= 0)[None, :] & ((key_entry != global_block)[None, :] | (key_pos[None, :] <= query_pos[:, None]))
    group_heads = min(HEADS, 8)
    group_count = HEADS // group_heads

    def per_group(index):
        part_query = lax.dynamic_slice_in_dim(queries, index * group_heads, group_heads, 1)
        part_keys = lax.dynamic_slice_in_dim(keys, index * group_heads, group_heads, 1)
        part_values = lax.dynamic_slice_in_dim(values, index * group_heads, group_heads, 1)
        scores = jnp.einsum('qhd,khd->hqk', part_query.astype(jnp.float32), part_keys.astype(jnp.float32))
        scores = jnp.where(allowed[None], scores, -jnp.inf)
        maxima = lax.optimization_barrier(jnp.max(scores, axis=-1, keepdims=True))
        raw = jnp.exp(scores - maxima)
        totals = lax.optimization_barrier(jnp.sum(raw, axis=-1))
        weights = raw.astype(jnp.bfloat16)
        context = jnp.einsum('hqk,khd->qhd', weights.astype(jnp.float32), part_values.astype(jnp.float32))
        return context / jnp.transpose(totals)[:, :, None]
    contexts = lax.map(per_group, jnp.arange(group_count, dtype=jnp.int32))
    contexts = jnp.transpose(contexts, (1, 0, 2, 3)).reshape(BLOCK, WIDTH)
    return (query_rows.astype(jnp.float32) + gain_out * contexts).astype(jnp.bfloat16)

def section_layer(earlier, current, block_list, gain_query, gain_key, gain_out):
    blocks_all = jnp.concatenate([earlier, current], 0).reshape(2 * NQ, BLOCK, WIDTH)
    current_blocks = current.reshape(NQ, BLOCK, WIDTH)

    def one_block(query_block):
        entries = block_list[query_block]
        picked = jnp.take(blocks_all, jnp.maximum(entries, 0).astype(jnp.int32), axis=0)
        return attend_block(current_blocks[query_block], picked, entries, NQ + query_block, gain_query, gain_key, gain_out)
    results = lax.map(one_block, jnp.arange(NQ, dtype=jnp.int32))
    return results.reshape(SPAN, WIDTH)

def reference(earlier_span, span_inputs, next_inputs, block_list, q_gain, k_gain, out_gain):
    first_out = []
    for section_id in range(SECTIONS - 1):
        first_out.append(section_layer(earlier_span[section_id], span_inputs[section_id], block_list, q_gain[section_id], k_gain[section_id], out_gain[section_id]))
    second_out = []
    for section_id in range(SECTIONS):
        incoming = next_inputs if section_id == 0 else first_out[section_id - 1]
        second_out.append(section_layer(span_inputs[section_id], incoming, block_list, q_gain[section_id], k_gain[section_id], out_gain[section_id]))
    return jnp.stack(second_out)
```

```python
import functools

import jax
import jax.numpy as jnp
from jax import lax
from jax.experimental import pallas as pl
from jax.experimental.pallas import tpu as pltpu
from jax.sharding import PartitionSpec as P

HEADS = 32
HD = 128
BLOCK = 128
LOCAL = 2
WIDTH = 4096
CHUNKS = 4
CHUNK = WIDTH // CHUNKS
HALF = CHUNK // 2
OUTER = 4
MESH = pl.DeviceIdType.MESH

A_S, A_R, YR_S, YR_R, YL_S, YL_R, ZR_S, ZR_R, ZL_S, ZL_R, C_S, C_R = range(12)
ROWS = 12


def kernel(
    n, sections, r_ref, early_ref, cur_ref, next_ref, gq_ref, gk_ref, go_ref, out_ref,
    second, first, prev, res, abuf, ycand, yfl, yfr, ysr, ysl, zcand, zfl, zfr, zsr, zsl,
    sems, psems, hsems,
):
    inner = n // (2 * OUTER)
    p = lax.axis_index("ctx")
    s = lax.axis_index("section")
    core = p % 2
    peer = p + 1 - 2 * core
    yi = (p // 2) % inner
    zi = p // (2 * inner)
    ystride, zstride = 2, 2 * inner
    after, before = lax.rem(p + 1, n), lax.rem(p + n - 1, n)
    r = r_ref[0]
    rc, ry, rz = r % 2, (r // 2) % inner, r // (2 * inner)
    later_ok = r + LOCAL <= p
    sends = s < sections - 1
    is_last = p == n - 1

    barrier = pltpu.get_barrier_semaphore()

    def greet(target):
        pl.semaphore_signal(barrier, inc=1, device_id=target, device_id_type=MESH)

    greet({"ctx": peer})
    greet({"ctx": after})
    greet({"ctx": before})
    total = jnp.int32(3)
    for there, axis, target in (
        (yi > 0, "ctx", p - ystride), (yi < inner - 1, "ctx", p + ystride),
        (zi > 0, "ctx", p - zstride), (zi < OUTER - 1, "ctx", p + zstride),
        (s > 0, "section", s - 1), (s < sections - 1, "section", s + 1),
    ):
        @pl.when(there)
        def _(axis=axis, target=target):
            greet({axis: target})
        total = total + there.astype(jnp.int32)
    pl.semaphore_wait(barrier, total)

    def cols(k):
        return pl.ds(pl.multiple_of(k * CHUNK, CHUNK), CHUNK)

    def half(k, c):
        return pl.ds(pl.multiple_of(k * CHUNK + c * HALF, HALF), HALF)

    def remote(src, dst, send, recv, target):
        return pltpu.make_async_remote_copy(
            src_ref=src, dst_ref=dst, send_sem=send, recv_sem=recv,
            device_id=target, device_id_type=MESH,
        )

    def swap_in(b, k, src):
        return remote(src.at[:, half(k, 1 - core)], abuf.at[b, k],
                      sems.at[A_S, b, k], sems.at[A_R, b, k], {"ctx": peer})

    def swap_out(b, k):
        part = res.at[b, :, half(k, core)]
        return remote(part, part, sems.at[C_S, b, k], sems.at[C_R, b, k], {"ctx": peer})

    def behind(b, k, src):
        return remote(src.at[:, cols(k)], prev.at[b, :, cols(k)],
                      psems.at[0, b, k], psems.at[1, b, k], {"ctx": after})

    def handoff(k):
        return remote(first.at[:, cols(k)], second.at[:, cols(k)],
                      hsems.at[0, k], hsems.at[1, k], {"section": lax.rem(s + 1, sections)})

    class Chain:
        def __init__(self, j, length, t, stride, cand, fl, fr, sr, sl, row):
            self.j, self.length, self.t, self.stride = j, length, t, stride
            self.cand, self.fl, self.fr, self.sr, self.sl, self.row = cand, fl, fr, sr, sl, row

        def right(self, b, k, src):
            return remote(src.at[b, k], self.fl.at[b, k], sems.at[self.row, b, k],
                          sems.at[self.row + 1, b, k], {"ctx": lax.rem(p + self.stride, n)})

        def left(self, b, k, src):
            return remote(src.at[b, k], self.fr.at[b, k], sems.at[self.row + 2, b, k],
                          sems.at[self.row + 3, b, k], {"ctx": lax.rem(p + n - self.stride, n)})

        def begin(self, b, k):
            @pl.when(self.j == 0)
            def _():
                self.right(b, k, self.cand).start()

            @pl.when(self.j == self.length - 1)
            def _():
                self.left(b, k, self.cand).start()

        def go_right(self, b, k):
            self.right(b, k, self.cand).wait_recv()

            @pl.when(self.j < self.length - 1)
            def _():
                self.sr[b, k] = jnp.where(self.t < self.j, self.fl[b, k], self.cand[b, k])
                self.right(b, k, self.sr).start()

        def go_left(self, b, k):
            self.left(b, k, self.cand).wait_recv()

            @pl.when(self.j > 0)
            def _():
                self.sl[b, k] = jnp.where(self.t > self.j, self.fr[b, k], self.cand[b, k])
                self.left(b, k, self.sl).start()

        def relay(self, b, k, store):
            j, t = self.j, self.t
            low = j < self.length // 2

            @pl.when(low)
            def _():
                @pl.when(j > 0)
                def _():
                    self.go_right(b, k)
                self.go_left(b, k)

            @pl.when(jnp.logical_not(low))
            def _():
                @pl.when(j < self.length - 1)
                def _():
                    self.go_left(b, k)
                self.go_right(b, k)

            @pl.when(j == 0)
            def _():
                store(jnp.where(t > j, self.fr[b, k], self.cand[b, k]))

            @pl.when(j == self.length - 1)
            def _():
                store(jnp.where(t < j, self.fl[b, k], self.cand[b, k]))

            @pl.when((j > 0) & (j < self.length - 1))
            def _():
                kept = jnp.where(t > j, self.fr[b, k], self.cand[b, k])
                store(jnp.where(t < j, self.fl[b, k], kept))

        def drain(self, b, k):
            @pl.when(self.j < self.length - 1)
            def _():
                self.right(b, k, self.cand).wait_send()

            @pl.when(self.j > 0)
            def _():
                self.left(b, k, self.cand).wait_send()

    ychain = Chain(yi, inner, ry, ystride, ycand, yfl, yfr, ysr, ysl, YR_S)
    zchain = Chain(zi, OUTER, rz, zstride, zcand, zfl, zfr, zsr, zsl, ZR_S)

    def stage_select(b, k, src):
        swap_in(b, k, src).wait_recv()
        ycand[b, k] = jnp.where(rc == core, src[:, half(k, core)], abuf[b, k])
        ychain.begin(b, k)

    def stage_y(b, k):
        def store(value):
            zcand[b, k] = value
        ychain.relay(b, k, store)
        zchain.begin(b, k)

    def stage_z(b, k):
        def store(value):
            res[b, :, half(k, core)] = value
        zchain.relay(b, k, store)
        swap_out(b, k).start()

    def drain(b, k, src):
        swap_in(b, k, src).wait_send()
        ychain.drain(b, k)
        zchain.drain(b, k)
        swap_out(b, k).wait_send()

    causal = (lax.broadcasted_iota(jnp.int32, (BLOCK, BLOCK), 1)
              <= lax.broadcasted_iota(jnp.int32, (BLOCK, BLOCK), 0))

    def normed(rows):
        wide = rows.astype(jnp.float32)
        return wide * lax.rsqrt(jnp.mean(wide * wide, axis=-1, keepdims=True) + 1e-06)

    def attend(k, query_ref, before_at, early_at, later_at, to_ref):
        def head(h, carry):
            at = pl.ds(pl.multiple_of(k * CHUNK + h * HD, HD), HD)
            gk = gk_ref[:, at]
            own = query_ref[:, at]
            rest = [prev[before_at, :, at], res[early_at, :, at], res[later_at, :, at]]
            own_n = normed(own)
            q = (own_n * gq_ref[:, at] * HD ** (-0.5)).astype(jnp.bfloat16)
            keys = [(own_n * gk).astype(jnp.bfloat16)]
            keys += [(normed(x) * gk).astype(jnp.bfloat16) for x in rest]
            keys = jnp.concatenate(keys, axis=0)
            values = jnp.concatenate([own] + rest, axis=0)
            sc = lax.dot_general(q, keys, (((1,), (1,)), ((), ())),
                                 preferred_element_type=jnp.float32)
            s0 = jnp.where(causal, sc[:, :BLOCK], -jnp.inf)
            s1 = sc[:, BLOCK:2 * BLOCK]
            s2 = sc[:, 2 * BLOCK:3 * BLOCK]
            s3 = jnp.where(later_ok, sc[:, 3 * BLOCK:], -jnp.inf)
            top = jnp.max(jnp.maximum(jnp.maximum(s0, s1), jnp.maximum(s2, s3)),
                          axis=-1, keepdims=True)
            raw = [jnp.exp(x - top) for x in (s0, s1, s2, s3)]
            tot = jnp.sum((raw[0] + raw[1]) + (raw[2] + raw[3]), axis=-1, keepdims=True)
            weights = jnp.concatenate([x.astype(jnp.bfloat16) for x in raw], axis=1)
            context = jnp.dot(weights, values, preferred_element_type=jnp.float32)
            to_ref[:, at] = (own.astype(jnp.float32)
                             + go_ref[:, at] * (context / tot)).astype(jnp.bfloat16)
            return carry
        lax.fori_loop(0, CHUNK // HD, head, 0)

    def each(count, body):
        def step(k, carry):
            body(k)
            return carry
        lax.fori_loop(0, count, step, 0)

    def staged(lag, t, body):
        k = t - lag

        @pl.when((k >= 0) & (k < CHUNKS))
        def _():
            body(jnp.clip(k, 0, CHUNKS - 1))

    def open_first(k):
        @pl.when(sends)
        def _():
            swap_in(0, k, early_ref).start()
        swap_in(1, k, cur_ref).start()

        @pl.when(sends & is_last)
        def _():
            behind(0, k, early_ref).start()

        @pl.when(sends & jnp.logical_not(is_last))
        def _():
            behind(0, k, cur_ref).start()

        @pl.when(s == 0)
        def _():
            second[:, cols(k)] = next_ref[:, cols(k)]

    each(CHUNKS, open_first)

    def both(stage, k, *src):
        @pl.when(sends)
        def _():
            stage(0, k, *src[:1])
        stage(1, k, *src[1:])

    def finish_first(k):
        swap_out(1, k).wait_recv()

        @pl.when(sends)
        def _():
            swap_out(0, k).wait_recv()
            behind(0, k, cur_ref).wait_recv()
            attend(k, cur_ref, 0, 0, 1, first)
            handoff(k).start()

    def first_step(t):
        staged(0, t, lambda k: both(stage_select, k, early_ref, cur_ref))
        staged(1, t, lambda k: both(stage_y, k))
        staged(2, t, lambda k: both(stage_z, k))
        staged(3, t, finish_first)

    each(CHUNKS + 3, first_step)

    def open_second(k):
        @pl.when(s > 0)
        def _():
            handoff(k).wait_recv()
        swap_in(2, k, second).start()

        @pl.when(is_last)
        def _():
            behind(1, k, cur_ref).start()

        @pl.when(jnp.logical_not(is_last))
        def _():
            behind(1, k, second).start()

    def finish_second(k):
        swap_out(2, k).wait_recv()
        behind(1, k, second).wait_recv()
        attend(k, second, 1, 1, 2, out_ref)

    def second_step(t):
        staged(0, t, open_second)
        staged(1, t, lambda k: stage_select(2, k, second))
        staged(2, t, lambda k: stage_y(2, k))
        staged(3, t, lambda k: stage_z(2, k))
        staged(4, t, finish_second)

    each(CHUNKS + 4, second_step)

    def close(k):
        @pl.when(sends)
        def _():
            drain(0, k, early_ref)
            behind(0, k, cur_ref).wait_send()
            handoff(k).wait_send()
        drain(1, k, cur_ref)
        drain(2, k, second)
        behind(1, k, second).wait_send()

    each(CHUNKS, close)


def local(earlier_span, span_inputs, next_inputs, block_list, q_gain, k_gain, out_gain):
    n = lax.axis_size("ctx")
    sections = lax.axis_size("section")
    r = lax.dynamic_slice(block_list, (n - 1, LOCAL), (1, 1)).reshape(1)
    piece = (3, CHUNKS, BLOCK, HALF)
    vmem = pl.BlockSpec(memory_space=pltpu.VMEM)
    result = pl.pallas_call(
        functools.partial(kernel, n, sections),
        out_shape=jax.ShapeDtypeStruct((BLOCK, WIDTH), jnp.bfloat16),
        in_specs=[pl.BlockSpec(memory_space=pltpu.SMEM)] + [vmem] * 6,
        out_specs=vmem,
        scratch_shapes=[
            pltpu.VMEM((BLOCK, WIDTH), jnp.bfloat16),
            pltpu.VMEM((BLOCK, WIDTH), jnp.bfloat16),
            pltpu.VMEM((2, BLOCK, WIDTH), jnp.bfloat16),
            pltpu.VMEM((3, BLOCK, WIDTH), jnp.bfloat16),
        ] + [pltpu.VMEM(piece, jnp.bfloat16)] * 11 + [
            pltpu.SemaphoreType.DMA((ROWS, 3, CHUNKS)),
            pltpu.SemaphoreType.DMA((2, 2, CHUNKS)),
            pltpu.SemaphoreType.DMA((2, CHUNKS)),
        ],
        compiler_params=pltpu.CompilerParams(
            collective_id=0, has_side_effects=True, vmem_limit_bytes=48 * 1024 * 1024,
        ),
    )(r, earlier_span[0], span_inputs[0], next_inputs, q_gain, k_gain, out_gain)
    return result[None]


def solution(mesh):
    in_specs = (
        P("section", "ctx", None),
        P("section", "ctx", None),
        P("ctx", None),
        P(),
        P("section", None),
        P("section", None),
        P("section", None),
    )
    out_specs = P("section", "ctx", None)
    return jax.shard_map(local, mesh=mesh, in_specs=in_specs, out_specs=out_specs, check_vma=False)
```

```python
import functools

import jax
import jax.numpy as jnp
from jax import lax
from jax.experimental import pallas as pl
from jax.experimental.pallas import tpu as pltpu
from jax.sharding import PartitionSpec as P

HEADS = 32
HD = 128
BLOCK = 128
LOCAL = 2
WIDTH = 4096
CHUNKS = 16
LAG = 2
CHUNK = WIDTH // CHUNKS
HALF = CHUNK // 2
OUTER = 4
MESH = pl.DeviceIdType.MESH

A_S, A_R, YR_S, YR_R, YL_S, YL_R, ZR_S, ZR_R, ZL_S, ZL_R, C_S, C_R = range(12)
ROWS = 12


def kernel(
    n, sections, list_ref, early_in, cur_in, next_in, gq_ref, gk_ref, go_ref, out_ref,
    early_ref, cur_ref, second, first, prev, res, abuf, ycand, yfl, yfr, ysr, ysl, zcand, zfl, zfr, zsr, zsl,
    sems, psems, hsems, lsems,
):
    inner = n // (2 * OUTER)
    p = lax.axis_index("ctx")
    s = lax.axis_index("section")
    core = p % 2
    peer = p + 1 - 2 * core
    yi = (p // 2) % inner
    zi = p // (2 * inner)
    ystride, zstride = 2, 2 * inner
    after, before = lax.rem(p + 1, n), lax.rem(p + n - 1, n)
    r = list_ref[n - 1, LOCAL]
    rc, ry, rz = r % 2, (r // 2) % inner, r // (2 * inner)
    later_ok = r + LOCAL <= p
    sends = s < sections - 1
    is_last = p == n - 1

    fetch_early = pltpu.make_async_copy(early_in.at[0], early_ref, lsems.at[0])
    fetch_cur = pltpu.make_async_copy(cur_in.at[0], cur_ref, lsems.at[1])
    fetch_next = pltpu.make_async_copy(next_in, second, lsems.at[2])
    fetch_early.start()
    fetch_cur.start()

    @pl.when(s == 0)
    def _():
        fetch_next.start()

    barrier = pltpu.get_barrier_semaphore()

    def greet(target):
        pl.semaphore_signal(barrier, inc=1, device_id=target, device_id_type=MESH)

    greet({"ctx": peer})
    greet({"ctx": after})
    greet({"ctx": before})
    total = jnp.int32(3)
    for there, axis, target in (
        (yi > 0, "ctx", p - ystride), (yi < inner - 1, "ctx", p + ystride),
        (zi > 0, "ctx", p - zstride), (zi < OUTER - 1, "ctx", p + zstride),
        (s > 0, "section", s - 1), (s < sections - 1, "section", s + 1),
    ):
        @pl.when(there)
        def _(axis=axis, target=target):
            greet({axis: target})
        total = total + there.astype(jnp.int32)
    pl.semaphore_wait(barrier, total)
    fetch_early.wait()
    fetch_cur.wait()

    def cols(k):
        return pl.ds(pl.multiple_of(k * CHUNK, CHUNK), CHUNK)

    def half(k, c):
        return pl.ds(pl.multiple_of(k * CHUNK + c * HALF, HALF), HALF)

    def remote(src, dst, send, recv, target):
        return pltpu.make_async_remote_copy(
            src_ref=src, dst_ref=dst, send_sem=send, recv_sem=recv,
            device_id=target, device_id_type=MESH,
        )

    def swap_in(b, k, src):
        return remote(src.at[:, half(k, 1 - core)], abuf.at[b, k],
                      sems.at[A_S, b, k], sems.at[A_R, b, k], {"ctx": peer})

    def swap_out(b, k):
        part = res.at[b, :, half(k, core)]
        return remote(part, part, sems.at[C_S, b, k], sems.at[C_R, b, k], {"ctx": peer})

    def behind(b, k, src):
        return remote(src.at[:, cols(k)], prev.at[b, :, cols(k)],
                      psems.at[0, b, k], psems.at[1, b, k], {"ctx": after})

    def handoff(k):
        return remote(first.at[:, cols(k)], second.at[:, cols(k)],
                      hsems.at[0, k], hsems.at[1, k], {"section": lax.rem(s + 1, sections)})

    def each(count, body):
        def step(k, carry):
            body(k)
            return carry
        lax.fori_loop(0, count, step, 0)

    def staged(lag, t, body):
        k = t - lag

        @pl.when((k >= 0) & (k < CHUNKS))
        def _():
            body(jnp.clip(k, 0, CHUNKS - 1))

    class Chain:
        def __init__(self, j, length, t, stride, cand, fl, fr, sr, sl, row):
            self.j, self.length, self.t, self.stride = j, length, t, stride
            self.cand, self.fl, self.fr, self.sr, self.sl, self.row = cand, fl, fr, sr, sl, row

        def right(self, b, k, src):
            return remote(src.at[b, k], self.fl.at[b, k], sems.at[self.row, b, k],
                          sems.at[self.row + 1, b, k], {"ctx": lax.rem(p + self.stride, n)})

        def left(self, b, k, src):
            return remote(src.at[b, k], self.fr.at[b, k], sems.at[self.row + 2, b, k],
                          sems.at[self.row + 3, b, k], {"ctx": lax.rem(p + n - self.stride, n)})

        def begin(self, b, k):
            @pl.when(self.j == 0)
            def _():
                self.right(b, k, self.cand).start()

            @pl.when(self.j == self.length - 1)
            def _():
                self.left(b, k, self.cand).start()

        def go_right(self, b, k):
            self.right(b, k, self.cand).wait_recv()
            self.sr[b, k] = jnp.where(self.t < self.j, self.fl[b, k], self.cand[b, k])
            self.right(b, k, self.sr).start()

        def go_left(self, b, k):
            self.left(b, k, self.cand).wait_recv()
            self.sl[b, k] = jnp.where(self.t > self.j, self.fr[b, k], self.cand[b, k])
            self.left(b, k, self.sl).start()

        def relay(self, t, lag, items):
            j, last = self.j, self.length - 1
            inside = (j > 0) & (j < last)

            def run(go):
                def body(k):
                    for there, b in items:
                        @pl.when(there & inside)
                        def _(b=b):
                            go(b, k)
                return body

            if self.length > 2:
                staged(lag + j * LAG, t, run(self.go_right))
                staged(lag + (last - j) * LAG, t, run(self.go_left))

        def finish(self, b, k, store):
            j, t, last = self.j, self.t, self.length - 1

            @pl.when(j == 0)
            def _():
                self.left(b, k, self.cand).wait_recv()
                store(jnp.where(t > j, self.fr[b, k], self.cand[b, k]))

            @pl.when(j == last)
            def _():
                self.right(b, k, self.cand).wait_recv()
                store(jnp.where(t < j, self.fl[b, k], self.cand[b, k]))

            if last > 1:
                @pl.when((j > 0) & (j < last))
                def _():
                    kept = jnp.where(t > j, self.fr[b, k], self.cand[b, k])
                    store(jnp.where(t < j, self.fl[b, k], kept))

        def drain(self, b, k):
            @pl.when(self.j < self.length - 1)
            def _():
                self.right(b, k, self.cand).wait_send()

            @pl.when(self.j > 0)
            def _():
                self.left(b, k, self.cand).wait_send()

    ychain = Chain(yi, inner, ry, ystride, ycand, yfl, yfr, ysr, ysl, YR_S)
    zchain = Chain(zi, OUTER, rz, zstride, zcand, zfl, zfr, zsr, zsl, ZR_S)

    def stage_select(b, k, src):
        swap_in(b, k, src).wait_recv()
        ycand[b, k] = jnp.where(rc == core, src[:, half(k, core)], abuf[b, k])
        ychain.begin(b, k)

    def stage_y(b, k):
        def store(value):
            zcand[b, k] = value
        ychain.finish(b, k, store)
        zchain.begin(b, k)

    def stage_z(b, k):
        def store(value):
            res[b, :, half(k, core)] = value
        zchain.finish(b, k, store)
        swap_out(b, k).start()

    def drain(b, k, src):
        swap_in(b, k, src).wait_send()
        ychain.drain(b, k)
        zchain.drain(b, k)
        swap_out(b, k).wait_send()

    causal = (lax.broadcasted_iota(jnp.int32, (BLOCK, BLOCK), 1)
              <= lax.broadcasted_iota(jnp.int32, (BLOCK, BLOCK), 0))

    def normed(rows):
        wide = rows.astype(jnp.float32)
        return wide * lax.rsqrt(jnp.mean(wide * wide, axis=-1, keepdims=True) + 1e-06)

    def attend(k, query_ref, before_at, early_at, later_at, to_ref):
        def head(h, carry):
            at = pl.ds(pl.multiple_of(k * CHUNK + h * HD, HD), HD)
            gk = gk_ref[:, at]
            own = query_ref[:, at]
            rest = [prev[before_at, :, at], res[early_at, :, at], res[later_at, :, at]]
            own_n = normed(own)
            q = (own_n * gq_ref[:, at] * HD ** (-0.5)).astype(jnp.bfloat16)
            keys = [(own_n * gk).astype(jnp.bfloat16)]
            keys += [(normed(x) * gk).astype(jnp.bfloat16) for x in rest]
            keys = jnp.concatenate(keys, axis=0)
            values = jnp.concatenate([own] + rest, axis=0)
            sc = lax.dot_general(q, keys, (((1,), (1,)), ((), ())),
                                 preferred_element_type=jnp.float32)
            s0 = jnp.where(causal, sc[:, :BLOCK], -jnp.inf)
            s1 = sc[:, BLOCK:2 * BLOCK]
            s2 = sc[:, 2 * BLOCK:3 * BLOCK]
            s3 = jnp.where(later_ok, sc[:, 3 * BLOCK:], -jnp.inf)
            top = jnp.max(jnp.maximum(jnp.maximum(s0, s1), jnp.maximum(s2, s3)),
                          axis=-1, keepdims=True)
            raw = [jnp.exp(x - top) for x in (s0, s1, s2, s3)]
            tot = jnp.sum((raw[0] + raw[1]) + (raw[2] + raw[3]), axis=-1, keepdims=True)
            weights = jnp.concatenate([x.astype(jnp.bfloat16) for x in raw], axis=1)
            context = jnp.dot(weights, values, preferred_element_type=jnp.float32)
            to_ref[:, at] = (own.astype(jnp.float32)
                             + go_ref[:, at] * (context / tot)).astype(jnp.bfloat16)
            return carry
        lax.fori_loop(0, CHUNK // HD, head, 0, unroll=min(4, CHUNK // HD))

    def open_first(k):
        @pl.when(sends)
        def _():
            swap_in(0, k, early_ref).start()
        swap_in(1, k, cur_ref).start()

        @pl.when(sends & is_last)
        def _():
            behind(0, k, early_ref).start()

        @pl.when(sends & jnp.logical_not(is_last))
        def _():
            behind(0, k, cur_ref).start()

    each(CHUNKS, open_first)

    @pl.when(s == 0)
    def _():
        fetch_next.wait()

    def both(stage, k, *src):
        @pl.when(sends)
        def _():
            stage(0, k, *src[:1])
        stage(1, k, *src[1:])

    def finish_first(k):
        swap_out(1, k).wait_recv()

        @pl.when(sends)
        def _():
            swap_out(0, k).wait_recv()
            behind(0, k, cur_ref).wait_recv()
            attend(k, cur_ref, 0, 0, 1, first)
            handoff(k).start()

    def open_second(k):
        @pl.when(s > 0)
        def _():
            handoff(k).wait_recv()
        swap_in(2, k, second).start()

        @pl.when(is_last)
        def _():
            behind(1, k, cur_ref).start()

        @pl.when(jnp.logical_not(is_last))
        def _():
            behind(1, k, second).start()

    def finish_second(k):
        swap_out(2, k).wait_recv()
        behind(1, k, second).wait_recv()
        attend(k, second, 1, 1, 2, out_ref.at[0])

    spread = (inner - 1) * LAG
    span = (OUTER - 1) * LAG
    early_item = [(sends, 0), (s >= 0, 1)]
    late_item = [(s >= 0, 2)]
    first_y = spread
    first_z = first_y + span
    first_end = first_z + LAG
    open_at = first_end + LAG
    pick_at = open_at + 1
    second_y = pick_at + spread
    second_z = second_y + span
    second_end = second_z + LAG

    def step(t):
        staged(0, t, lambda k: both(stage_select, k, early_ref, cur_ref))
        ychain.relay(t, 0, early_item)
        staged(first_y, t, lambda k: both(stage_y, k))
        zchain.relay(t, first_y, early_item)
        staged(first_z, t, lambda k: both(stage_z, k))
        staged(open_at, t, open_second)
        staged(pick_at, t, lambda k: stage_select(2, k, second))
        ychain.relay(t, pick_at, late_item)
        staged(second_y, t, lambda k: stage_y(2, k))
        zchain.relay(t, second_y, late_item)
        staged(second_z, t, lambda k: stage_z(2, k))
        staged(first_end, t, finish_first)
        staged(second_end, t, finish_second)

    each(CHUNKS + second_end, step)

    def close(k):
        @pl.when(sends)
        def _():
            drain(0, k, early_ref)
            behind(0, k, cur_ref).wait_send()
            handoff(k).wait_send()
        drain(1, k, cur_ref)
        drain(2, k, second)
        behind(1, k, second).wait_send()

    each(CHUNKS, close)


def local(earlier_span, span_inputs, next_inputs, block_list, q_gain, k_gain, out_gain):
    n = lax.axis_size("ctx")
    sections = lax.axis_size("section")
    piece = (3, CHUNKS, BLOCK, HALF)
    vmem = pl.BlockSpec(memory_space=pltpu.VMEM)
    return pl.pallas_call(
        functools.partial(kernel, n, sections),
        out_shape=jax.ShapeDtypeStruct((1, BLOCK, WIDTH), jnp.bfloat16),
        in_specs=[pl.BlockSpec(memory_space=pltpu.SMEM)] + [pl.BlockSpec(memory_space=pl.ANY)] * 3 + [vmem] * 3,
        out_specs=vmem,
        scratch_shapes=[pltpu.VMEM((BLOCK, WIDTH), jnp.bfloat16)] * 4 + [
            pltpu.VMEM((2, BLOCK, WIDTH), jnp.bfloat16),
            pltpu.VMEM((3, BLOCK, WIDTH), jnp.bfloat16),
        ] + [pltpu.VMEM(piece, jnp.bfloat16)] * 11 + [
            pltpu.SemaphoreType.DMA((ROWS, 3, CHUNKS)),
            pltpu.SemaphoreType.DMA((2, 2, CHUNKS)),
            pltpu.SemaphoreType.DMA((2, CHUNKS)),
            pltpu.SemaphoreType.DMA((3,)),
        ],
        compiler_params=pltpu.CompilerParams(
            collective_id=0, has_side_effects=True, vmem_limit_bytes=48 * 1024 * 1024,
        ),
    )(block_list, earlier_span, span_inputs, next_inputs, q_gain, k_gain, out_gain)


def solution(mesh):
    in_specs = (
        P("section", "ctx", None),
        P("section", "ctx", None),
        P("ctx", None),
        P(),
        P("section", None),
        P("section", None),
        P("section", None),
    )
    out_specs = P("section", "ctx", None)
    return jax.shard_map(local, mesh=mesh, in_specs=in_specs, out_specs=out_specs, check_vma=False)
```

```python
import functools

import jax
import jax.numpy as jnp
from jax import lax
from jax.experimental import pallas as pl
from jax.experimental.pallas import tpu as pltpu
from jax.sharding import PartitionSpec as P

HEADS = 32
HD = 128
BLOCK = 128
LOCAL = 2
WIDTH = 4096
CHUNKS = 16
LAG = 2
BEFORE = 3
CHUNK = WIDTH // CHUNKS
HALF = CHUNK // 2
OUTER = 4
MESH = pl.DeviceIdType.MESH

A_S, A_R, YR_S, YR_R, YL_S, YL_R, ZR_S, ZR_R, ZL_S, ZL_R, C_S, C_R = range(12)
ROWS = 12


def kernel(
    n, sections, list_ref, early_in, cur_in, next_in, gq_ref, gk_ref, go_ref, out_ref,
    early_ref, cur_ref, second, first, prev, res, abuf, ycand, yfl, yfr, ysr, ysl, zcand, zfl, zfr, zsr, zsl,
    sems, psems, hsems, lsems,
):
    inner = n // (2 * OUTER)
    p = lax.axis_index("ctx")
    s = lax.axis_index("section")
    core = p % 2
    peer = p + 1 - 2 * core
    yi = (p // 2) % inner
    zi = p // (2 * inner)
    ystride, zstride = 2, 2 * inner
    after, before = lax.rem(p + 1, n), lax.rem(p + n - 1, n)
    r = list_ref[n - 1, LOCAL]
    rc, ry, rz = r % 2, (r // 2) % inner, r // (2 * inner)
    later_ok = r + LOCAL <= p
    sends = s < sections - 1
    is_last = p == n - 1

    fetch_early = pltpu.make_async_copy(early_in.at[0], early_ref, lsems.at[0])
    fetch_cur = pltpu.make_async_copy(cur_in.at[0], cur_ref, lsems.at[1])
    fetch_next = pltpu.make_async_copy(next_in, second, lsems.at[2])
    fetch_early.start()
    fetch_cur.start()

    @pl.when(s == 0)
    def _():
        fetch_next.start()

    barrier = pltpu.get_barrier_semaphore()

    def greet(target):
        pl.semaphore_signal(barrier, inc=1, device_id=target, device_id_type=MESH)

    greet({"ctx": peer})
    greet({"ctx": after})
    greet({"ctx": before})
    total = jnp.int32(3)
    for there, axis, target in (
        (yi > 0, "ctx", p - ystride), (yi < inner - 1, "ctx", p + ystride),
        (zi > 0, "ctx", p - zstride), (zi < OUTER - 1, "ctx", p + zstride),
        (s > 0, "section", s - 1), (s < sections - 1, "section", s + 1),
    ):
        @pl.when(there)
        def _(axis=axis, target=target):
            greet({axis: target})
        total = total + there.astype(jnp.int32)
    pl.semaphore_wait(barrier, total)
    fetch_early.wait()
    fetch_cur.wait()

    def cols(k):
        return pl.ds(pl.multiple_of(k * CHUNK, CHUNK), CHUNK)

    def half(k, c):
        return pl.ds(pl.multiple_of(k * CHUNK + c * HALF, HALF), HALF)

    def remote(src, dst, send, recv, target):
        return pltpu.make_async_remote_copy(
            src_ref=src, dst_ref=dst, send_sem=send, recv_sem=recv,
            device_id=target, device_id_type=MESH,
        )

    def swap_in(b, k, src):
        return remote(src.at[:, half(k, 1 - core)], abuf.at[b, k],
                      sems.at[A_S, b, k], sems.at[A_R, b, k], {"ctx": peer})

    def swap_out(b, k):
        part = res.at[b, :, half(k, core)]
        return remote(part, part, sems.at[C_S, b, k], sems.at[C_R, b, k], {"ctx": peer})

    def behind(b, k, src):
        return remote(src.at[:, cols(k)], prev.at[b, :, cols(k)],
                      psems.at[0, b, k], psems.at[1, b, k], {"ctx": after})

    def handoff(k):
        return remote(first.at[:, cols(k)], second.at[:, cols(k)],
                      hsems.at[0, k], hsems.at[1, k], {"section": lax.rem(s + 1, sections)})

    def each(count, body):
        def step(k, carry):
            body(k)
            return carry
        lax.fori_loop(0, count, step, 0)

    def staged(lag, t, body):
        k = t - lag

        @pl.when((k >= 0) & (k < CHUNKS))
        def _():
            body(jnp.clip(k, 0, CHUNKS - 1))

    class Chain:
        def __init__(self, j, length, t, stride, cand, fl, fr, sr, sl, row):
            self.j, self.length, self.t, self.stride = j, length, t, stride
            self.cand, self.fl, self.fr, self.sr, self.sl, self.row = cand, fl, fr, sr, sl, row

        def right(self, b, k, src):
            return remote(src.at[b, k], self.fl.at[b, k], sems.at[self.row, b, k],
                          sems.at[self.row + 1, b, k], {"ctx": lax.rem(p + self.stride, n)})

        def left(self, b, k, src):
            return remote(src.at[b, k], self.fr.at[b, k], sems.at[self.row + 2, b, k],
                          sems.at[self.row + 3, b, k], {"ctx": lax.rem(p + n - self.stride, n)})

        def begin(self, b, k):
            @pl.when(self.j == 0)
            def _():
                self.right(b, k, self.cand).start()

            @pl.when(self.j == self.length - 1)
            def _():
                self.left(b, k, self.cand).start()

        def go_right(self, b, k):
            self.right(b, k, self.cand).wait_recv()
            self.sr[b, k] = jnp.where(self.t < self.j, self.fl[b, k], self.cand[b, k])
            self.right(b, k, self.sr).start()

        def go_left(self, b, k):
            self.left(b, k, self.cand).wait_recv()
            self.sl[b, k] = jnp.where(self.t > self.j, self.fr[b, k], self.cand[b, k])
            self.left(b, k, self.sl).start()

        def relay(self, t, lag, items):
            j, last = self.j, self.length - 1
            inside = (j > 0) & (j < last)

            def run(go):
                def body(k):
                    for there, b in items:
                        @pl.when(there & inside)
                        def _(b=b):
                            go(b, k)
                return body

            if self.length > 2:
                staged(lag + j * LAG, t, run(self.go_right))
                staged(lag + (last - j) * LAG, t, run(self.go_left))

        def finish(self, b, k, store):
            j, t, last = self.j, self.t, self.length - 1

            @pl.when(j == 0)
            def _():
                self.left(b, k, self.cand).wait_recv()
                store(jnp.where(t > j, self.fr[b, k], self.cand[b, k]))

            @pl.when(j == last)
            def _():
                self.right(b, k, self.cand).wait_recv()
                store(jnp.where(t < j, self.fl[b, k], self.cand[b, k]))

            if last > 1:
                @pl.when((j > 0) & (j < last))
                def _():
                    kept = jnp.where(t > j, self.fr[b, k], self.cand[b, k])
                    store(jnp.where(t < j, self.fl[b, k], kept))

        def drain(self, b, k):
            @pl.when(self.j < self.length - 1)
            def _():
                self.right(b, k, self.cand).wait_send()

            @pl.when(self.j > 0)
            def _():
                self.left(b, k, self.cand).wait_send()

    ychain = Chain(yi, inner, ry, ystride, ycand, yfl, yfr, ysr, ysl, YR_S)
    zchain = Chain(zi, OUTER, rz, zstride, zcand, zfl, zfr, zsr, zsl, ZR_S)

    def stage_select(b, k, src):
        swap_in(b, k, src).wait_recv()
        ycand[b, k] = jnp.where(rc == core, src[:, half(k, core)], abuf[b, k])
        ychain.begin(b, k)

    def stage_y(b, k):
        def store(value):
            zcand[b, k] = value
        ychain.finish(b, k, store)
        zchain.begin(b, k)

    def stage_z(b, k):
        def store(value):
            res[b, :, half(k, core)] = value
        zchain.finish(b, k, store)
        swap_out(b, k).start()

    def drain(b, k, src):
        swap_in(b, k, src).wait_send()
        ychain.drain(b, k)
        zchain.drain(b, k)
        swap_out(b, k).wait_send()

    causal = (lax.broadcasted_iota(jnp.int32, (BLOCK, BLOCK), 1)
              <= lax.broadcasted_iota(jnp.int32, (BLOCK, BLOCK), 0))

    def normed(rows):
        wide = rows.astype(jnp.float32)
        return wide * lax.rsqrt(jnp.mean(wide * wide, axis=-1, keepdims=True) + 1e-06)

    def attend(k, query_ref, before_at, early_at, later_at, to_ref):
        def head(h, carry):
            at = pl.ds(pl.multiple_of(k * CHUNK + h * HD, HD), HD)
            gk = gk_ref[:, at]
            own = query_ref[:, at]
            rest = [prev[before_at, :, at], res[early_at, :, at], res[later_at, :, at]]
            own_n = normed(own)
            q = (own_n * gq_ref[:, at] * HD ** (-0.5)).astype(jnp.bfloat16)
            keys = [(own_n * gk).astype(jnp.bfloat16)]
            keys += [(normed(x) * gk).astype(jnp.bfloat16) for x in rest]
            keys = jnp.concatenate(keys, axis=0)
            values = jnp.concatenate([own] + rest, axis=0)
            sc = lax.dot_general(q, keys, (((1,), (1,)), ((), ())),
                                 preferred_element_type=jnp.float32)
            s0 = jnp.where(causal, sc[:, :BLOCK], -jnp.inf)
            s1 = sc[:, BLOCK:2 * BLOCK]
            s2 = sc[:, 2 * BLOCK:3 * BLOCK]
            s3 = jnp.where(later_ok, sc[:, 3 * BLOCK:], -jnp.inf)
            top = jnp.max(jnp.maximum(jnp.maximum(s0, s1), jnp.maximum(s2, s3)),
                          axis=-1, keepdims=True)
            raw = [jnp.exp(x - top) for x in (s0, s1, s2, s3)]
            tot = jnp.sum((raw[0] + raw[1]) + (raw[2] + raw[3]), axis=-1, keepdims=True)
            weights = jnp.concatenate([x.astype(jnp.bfloat16) for x in raw], axis=1)
            context = jnp.dot(weights, values, preferred_element_type=jnp.float32)
            to_ref[:, at] = (own.astype(jnp.float32)
                             + go_ref[:, at] * (context / tot)).astype(jnp.bfloat16)
            return carry
        lax.fori_loop(0, CHUNK // HD, head, 0, unroll=min(4, CHUNK // HD))

    def open_first(k):
        @pl.when(sends)
        def _():
            swap_in(0, k, early_ref).start()
        swap_in(1, k, cur_ref).start()

    def open_before(k):
        @pl.when(sends & is_last)
        def _():
            behind(0, k, early_ref).start()

        @pl.when(sends & jnp.logical_not(is_last))
        def _():
            behind(0, k, cur_ref).start()

    each(CHUNKS, open_first)

    @pl.when(s == 0)
    def _():
        fetch_next.wait()

    def both(stage, k, *src):
        @pl.when(sends)
        def _():
            stage(0, k, *src[:1])
        stage(1, k, *src[1:])

    def finish_first(k):
        swap_out(1, k).wait_recv()

        @pl.when(sends)
        def _():
            swap_out(0, k).wait_recv()
            behind(0, k, cur_ref).wait_recv()
            attend(k, cur_ref, 0, 0, 1, first)
            handoff(k).start()

    def open_second(k):
        @pl.when(s > 0)
        def _():
            handoff(k).wait_recv()
        swap_in(2, k, second).start()

    def open_second_before(k):
        @pl.when(is_last)
        def _():
            behind(1, k, cur_ref).start()

        @pl.when(jnp.logical_not(is_last))
        def _():
            behind(1, k, second).start()

    def finish_second(k):
        swap_out(2, k).wait_recv()
        behind(1, k, second).wait_recv()
        attend(k, second, 1, 1, 2, out_ref.at[0])

    spread = (inner - 1) * LAG
    span = (OUTER - 1) * LAG
    early_item = [(sends, 0), (s >= 0, 1)]
    late_item = [(s >= 0, 2)]
    first_y = spread
    first_z = first_y + span
    first_end = first_z + LAG
    open_at = first_end + LAG
    pick_at = open_at + 1
    second_y = pick_at + spread
    second_z = second_y + span
    second_end = second_z + LAG

    def step(t):
        staged(0, t, lambda k: both(stage_select, k, early_ref, cur_ref))
        ychain.relay(t, 0, early_item)
        staged(BEFORE, t, open_before)
        staged(first_y, t, lambda k: both(stage_y, k))
        zchain.relay(t, first_y, early_item)
        staged(first_z, t, lambda k: both(stage_z, k))
        staged(open_at, t, open_second)
        staged(pick_at, t, lambda k: stage_select(2, k, second))
        staged(pick_at + BEFORE, t, open_second_before)
        ychain.relay(t, pick_at, late_item)
        staged(second_y, t, lambda k: stage_y(2, k))
        zchain.relay(t, second_y, late_item)
        staged(second_z, t, lambda k: stage_z(2, k))
        staged(first_end, t, finish_first)
        staged(second_end, t, finish_second)

    each(CHUNKS + second_end, step)

    def close(k):
        @pl.when(sends)
        def _():
            drain(0, k, early_ref)
            behind(0, k, cur_ref).wait_send()
            handoff(k).wait_send()
        drain(1, k, cur_ref)
        drain(2, k, second)
        behind(1, k, second).wait_send()

    each(CHUNKS, close)


def local(earlier_span, span_inputs, next_inputs, block_list, q_gain, k_gain, out_gain):
    n = lax.axis_size("ctx")
    sections = lax.axis_size("section")
    piece = (3, CHUNKS, BLOCK, HALF)
    vmem = pl.BlockSpec(memory_space=pltpu.VMEM)
    return pl.pallas_call(
        functools.partial(kernel, n, sections),
        out_shape=jax.ShapeDtypeStruct((1, BLOCK, WIDTH), jnp.bfloat16),
        in_specs=[pl.BlockSpec(memory_space=pltpu.SMEM)] + [pl.BlockSpec(memory_space=pl.ANY)] * 3 + [vmem] * 3,
        out_specs=vmem,
        scratch_shapes=[pltpu.VMEM((BLOCK, WIDTH), jnp.bfloat16)] * 4 + [
            pltpu.VMEM((2, BLOCK, WIDTH), jnp.bfloat16),
            pltpu.VMEM((3, BLOCK, WIDTH), jnp.bfloat16),
        ] + [pltpu.VMEM(piece, jnp.bfloat16)] * 11 + [
            pltpu.SemaphoreType.DMA((ROWS, 3, CHUNKS)),
            pltpu.SemaphoreType.DMA((2, 2, CHUNKS)),
            pltpu.SemaphoreType.DMA((2, CHUNKS)),
            pltpu.SemaphoreType.DMA((3,)),
        ],
        compiler_params=pltpu.CompilerParams(
            collective_id=0, has_side_effects=True, vmem_limit_bytes=48 * 1024 * 1024,
        ),
    )(block_list, earlier_span, span_inputs, next_inputs, q_gain, k_gain, out_gain)


def solution(mesh):
    in_specs = (
        P("section", "ctx", None),
        P("section", "ctx", None),
        P("ctx", None),
        P(),
        P("section", None),
        P("section", None),
        P("section", None),
    )
    out_specs = P("section", "ctx", None)
    return jax.shard_map(local, mesh=mesh, in_specs=in_specs, out_specs=out_specs, check_vma=False)
```

```python
import functools

import jax
import jax.numpy as jnp
from jax import lax
from jax.experimental import pallas as pl
from jax.experimental.pallas import tpu as pltpu
from jax.sharding import PartitionSpec as P

HEADS = 32
HD = 128
BLOCK = 128
LOCAL = 2
WIDTH = 4096
CHUNKS = 16
LAG = 2
BEFORE = 5
CHUNK = WIDTH // CHUNKS
HALF = CHUNK // 2
OUTER = 4
MESH = pl.DeviceIdType.MESH

A_S, A_R, YR_S, YR_R, YL_S, YL_R, ZR_S, ZR_R, ZL_S, ZL_R, C_S, C_R = range(12)
ROWS = 12


def kernel(
    n, sections, list_ref, early_in, cur_in, next_in, gq_ref, gk_ref, go_ref, out_ref,
    early_ref, cur_ref, second, first, prev, res, abuf, ycand, yfl, yfr, ysr, ysl, zcand, zfl, zfr, zsr, zsl,
    sems, psems, hsems, lsems,
):
    inner = n // (2 * OUTER)
    p = lax.axis_index("ctx")
    s = lax.axis_index("section")
    core = p % 2
    peer = p + 1 - 2 * core
    yi = (p // 2) % inner
    zi = p // (2 * inner)
    ystride, zstride = 2, 2 * inner
    after, before = lax.rem(p + 1, n), lax.rem(p + n - 1, n)
    r = list_ref[n - 1, LOCAL]
    rc, ry, rz = r % 2, (r // 2) % inner, r // (2 * inner)
    later_ok = r + LOCAL <= p
    sends = s < sections - 1
    is_last = p == n - 1

    fetch_early = pltpu.make_async_copy(early_in.at[0], early_ref, lsems.at[0])
    fetch_cur = pltpu.make_async_copy(cur_in.at[0], cur_ref, lsems.at[1])
    fetch_next = pltpu.make_async_copy(next_in, second, lsems.at[2])
    fetch_early.start()
    fetch_cur.start()

    @pl.when(s == 0)
    def _():
        fetch_next.start()

    barrier = pltpu.get_barrier_semaphore()

    def greet(target):
        pl.semaphore_signal(barrier, inc=1, device_id=target, device_id_type=MESH)

    greet({"ctx": peer})
    greet({"ctx": after})
    greet({"ctx": before})
    total = jnp.int32(3)
    for there, axis, target in (
        (yi > 0, "ctx", p - ystride), (yi < inner - 1, "ctx", p + ystride),
        (zi > 0, "ctx", p - zstride), (zi < OUTER - 1, "ctx", p + zstride),
        (s > 0, "section", s - 1), (s < sections - 1, "section", s + 1),
    ):
        @pl.when(there)
        def _(axis=axis, target=target):
            greet({axis: target})
        total = total + there.astype(jnp.int32)
    pl.semaphore_wait(barrier, total)
    fetch_early.wait()
    fetch_cur.wait()

    def cols(k):
        return pl.ds(pl.multiple_of(k * CHUNK, CHUNK), CHUNK)

    def half(k, c):
        return pl.ds(pl.multiple_of(k * CHUNK + c * HALF, HALF), HALF)

    def remote(src, dst, send, recv, target):
        return pltpu.make_async_remote_copy(
            src_ref=src, dst_ref=dst, send_sem=send, recv_sem=recv,
            device_id=target, device_id_type=MESH,
        )

    def swap_in(b, k, src):
        return remote(src.at[:, half(k, 1 - core)], abuf.at[b, k],
                      sems.at[A_S, b, k], sems.at[A_R, b, k], {"ctx": peer})

    def swap_out(b, k):
        part = res.at[b, :, half(k, core)]
        return remote(part, part, sems.at[C_S, b, k], sems.at[C_R, b, k], {"ctx": peer})

    def behind(b, k, src):
        return remote(src.at[:, cols(k)], prev.at[b, :, cols(k)],
                      psems.at[0, b, k], psems.at[1, b, k], {"ctx": after})

    def handoff(k):
        return remote(first.at[:, cols(k)], second.at[:, cols(k)],
                      hsems.at[0, k], hsems.at[1, k], {"section": lax.rem(s + 1, sections)})

    def each(count, body):
        def step(k, carry):
            body(k)
            return carry
        lax.fori_loop(0, count, step, 0)

    def staged(lag, t, body):
        k = t - lag

        @pl.when((k >= 0) & (k < CHUNKS))
        def _():
            body(jnp.clip(k, 0, CHUNKS - 1))

    class Chain:
        def __init__(self, j, length, t, stride, cand, fl, fr, sr, sl, row):
            self.j, self.length, self.t, self.stride = j, length, t, stride
            self.cand, self.fl, self.fr, self.sr, self.sl, self.row = cand, fl, fr, sr, sl, row

        def right(self, b, k, src):
            return remote(src.at[b, k], self.fl.at[b, k], sems.at[self.row, b, k],
                          sems.at[self.row + 1, b, k], {"ctx": lax.rem(p + self.stride, n)})

        def left(self, b, k, src):
            return remote(src.at[b, k], self.fr.at[b, k], sems.at[self.row + 2, b, k],
                          sems.at[self.row + 3, b, k], {"ctx": lax.rem(p + n - self.stride, n)})

        def begin(self, b, k):
            @pl.when(self.j == 0)
            def _():
                self.right(b, k, self.cand).start()

            @pl.when(self.j == self.length - 1)
            def _():
                self.left(b, k, self.cand).start()

        def go_right(self, b, k):
            self.right(b, k, self.cand).wait_recv()
            self.sr[b, k] = jnp.where(self.t < self.j, self.fl[b, k], self.cand[b, k])
            self.right(b, k, self.sr).start()

        def go_left(self, b, k):
            self.left(b, k, self.cand).wait_recv()
            self.sl[b, k] = jnp.where(self.t > self.j, self.fr[b, k], self.cand[b, k])
            self.left(b, k, self.sl).start()

        def relay(self, t, lag, items):
            j, last = self.j, self.length - 1
            inside = (j > 0) & (j < last)

            def run(go):
                def body(k):
                    for there, b in items:
                        @pl.when(there & inside)
                        def _(b=b):
                            go(b, k)
                return body

            if self.length > 2:
                staged(lag + j * LAG, t, run(self.go_right))
                staged(lag + (last - j) * LAG, t, run(self.go_left))

        def finish(self, b, k, store):
            j, t, last = self.j, self.t, self.length - 1

            @pl.when(j == 0)
            def _():
                self.left(b, k, self.cand).wait_recv()
                store(jnp.where(t > j, self.fr[b, k], self.cand[b, k]))

            @pl.when(j == last)
            def _():
                self.right(b, k, self.cand).wait_recv()
                store(jnp.where(t < j, self.fl[b, k], self.cand[b, k]))

            if last > 1:
                @pl.when((j > 0) & (j < last))
                def _():
                    kept = jnp.where(t > j, self.fr[b, k], self.cand[b, k])
                    store(jnp.where(t < j, self.fl[b, k], kept))

        def drain(self, b, k):
            @pl.when(self.j < self.length - 1)
            def _():
                self.right(b, k, self.cand).wait_send()

            @pl.when(self.j > 0)
            def _():
                self.left(b, k, self.cand).wait_send()

    ychain = Chain(yi, inner, ry, ystride, ycand, yfl, yfr, ysr, ysl, YR_S)
    zchain = Chain(zi, OUTER, rz, zstride, zcand, zfl, zfr, zsr, zsl, ZR_S)

    def stage_select(b, k, src):
        swap_in(b, k, src).wait_recv()
        ycand[b, k] = jnp.where(rc == core, src[:, half(k, core)], abuf[b, k])
        ychain.begin(b, k)

    def stage_y(b, k):
        def store(value):
            zcand[b, k] = value
        ychain.finish(b, k, store)
        zchain.begin(b, k)

    def stage_z(b, k):
        def store(value):
            res[b, :, half(k, core)] = value
        zchain.finish(b, k, store)
        swap_out(b, k).start()

    def drain(b, k, src):
        swap_in(b, k, src).wait_send()
        ychain.drain(b, k)
        zchain.drain(b, k)
        swap_out(b, k).wait_send()

    causal = (lax.broadcasted_iota(jnp.int32, (BLOCK, BLOCK), 1)
              <= lax.broadcasted_iota(jnp.int32, (BLOCK, BLOCK), 0))

    def normed(rows):
        wide = rows.astype(jnp.float32)
        return wide * lax.rsqrt(jnp.mean(wide * wide, axis=-1, keepdims=True) + 1e-06)

    def attend(k, query_ref, before_at, early_at, later_at, to_ref):
        def head(h, carry):
            at = pl.ds(pl.multiple_of(k * CHUNK + h * HD, HD), HD)
            gk = gk_ref[:, at]
            own = query_ref[:, at]
            rest = [prev[before_at, :, at], res[early_at, :, at], res[later_at, :, at]]
            own_n = normed(own)
            q = (own_n * gq_ref[:, at] * HD ** (-0.5)).astype(jnp.bfloat16)
            keys = [(own_n * gk).astype(jnp.bfloat16)]
            keys += [(normed(x) * gk).astype(jnp.bfloat16) for x in rest]
            keys = jnp.concatenate(keys, axis=0)
            values = jnp.concatenate([own] + rest, axis=0)
            sc = lax.dot_general(q, keys, (((1,), (1,)), ((), ())),
                                 preferred_element_type=jnp.float32)
            s0 = jnp.where(causal, sc[:, :BLOCK], -jnp.inf)
            s1 = sc[:, BLOCK:2 * BLOCK]
            s2 = sc[:, 2 * BLOCK:3 * BLOCK]
            s3 = jnp.where(later_ok, sc[:, 3 * BLOCK:], -jnp.inf)
            top = jnp.max(jnp.maximum(jnp.maximum(s0, s1), jnp.maximum(s2, s3)),
                          axis=-1, keepdims=True)
            raw = [jnp.exp(x - top) for x in (s0, s1, s2, s3)]
            tot = jnp.sum((raw[0] + raw[1]) + (raw[2] + raw[3]), axis=-1, keepdims=True)
            weights = jnp.concatenate([x.astype(jnp.bfloat16) for x in raw], axis=1)
            context = jnp.dot(weights, values, preferred_element_type=jnp.float32)
            to_ref[:, at] = (own.astype(jnp.float32)
                             + go_ref[:, at] * (context / tot)).astype(jnp.bfloat16)
            return carry
        lax.fori_loop(0, CHUNK // HD, head, 0, unroll=min(4, CHUNK // HD))

    def open_first(k):
        @pl.when(sends)
        def _():
            swap_in(0, k, early_ref).start()
        swap_in(1, k, cur_ref).start()

    def open_before(k):
        @pl.when(sends & is_last)
        def _():
            behind(0, k, early_ref).start()

        @pl.when(sends & jnp.logical_not(is_last))
        def _():
            behind(0, k, cur_ref).start()

    each(CHUNKS, open_first)

    @pl.when(s == 0)
    def _():
        fetch_next.wait()

    def both(stage, k, *src):
        @pl.when(sends)
        def _():
            stage(0, k, *src[:1])
        stage(1, k, *src[1:])

    def finish_first(k):
        swap_out(1, k).wait_recv()

        @pl.when(sends)
        def _():
            swap_out(0, k).wait_recv()
            behind(0, k, cur_ref).wait_recv()
            attend(k, cur_ref, 0, 0, 1, first)
            handoff(k).start()

    def open_second(k):
        @pl.when(s > 0)
        def _():
            handoff(k).wait_recv()
        swap_in(2, k, second).start()

    def open_second_before(k):
        @pl.when(is_last)
        def _():
            behind(1, k, cur_ref).start()

        @pl.when(jnp.logical_not(is_last))
        def _():
            behind(1, k, second).start()

    def finish_second(k):
        swap_out(2, k).wait_recv()
        behind(1, k, second).wait_recv()
        attend(k, second, 1, 1, 2, out_ref.at[0])

    spread = (inner - 1) * LAG
    span = (OUTER - 1) * LAG
    early_item = [(sends, 0), (s >= 0, 1)]
    late_item = [(s >= 0, 2)]
    first_y = spread
    first_z = first_y + span
    first_end = first_z + 1
    open_at = first_end + 1
    pick_at = open_at + 1
    second_y = pick_at + spread
    second_z = second_y + span
    second_end = second_z + 1

    def step(t):
        staged(0, t, lambda k: both(stage_select, k, early_ref, cur_ref))
        ychain.relay(t, 0, early_item)
        staged(BEFORE, t, open_before)
        staged(first_y, t, lambda k: both(stage_y, k))
        zchain.relay(t, first_y, early_item)
        staged(first_z, t, lambda k: both(stage_z, k))
        staged(open_at, t, open_second)
        staged(pick_at, t, lambda k: stage_select(2, k, second))
        staged(pick_at + BEFORE, t, open_second_before)
        ychain.relay(t, pick_at, late_item)
        staged(second_y, t, lambda k: stage_y(2, k))
        zchain.relay(t, second_y, late_item)
        staged(second_z, t, lambda k: stage_z(2, k))
        staged(first_end, t, finish_first)
        staged(second_end, t, finish_second)

    each(CHUNKS + second_end, step)

    def close(k):
        @pl.when(sends)
        def _():
            drain(0, k, early_ref)
            behind(0, k, cur_ref).wait_send()
            handoff(k).wait_send()
        drain(1, k, cur_ref)
        drain(2, k, second)
        behind(1, k, second).wait_send()

    each(CHUNKS, close)


def local(earlier_span, span_inputs, next_inputs, block_list, q_gain, k_gain, out_gain):
    n = lax.axis_size("ctx")
    sections = lax.axis_size("section")
    piece = (3, CHUNKS, BLOCK, HALF)
    vmem = pl.BlockSpec(memory_space=pltpu.VMEM)
    return pl.pallas_call(
        functools.partial(kernel, n, sections),
        out_shape=jax.ShapeDtypeStruct((1, BLOCK, WIDTH), jnp.bfloat16),
        in_specs=[pl.BlockSpec(memory_space=pltpu.SMEM)] + [pl.BlockSpec(memory_space=pl.ANY)] * 3 + [vmem] * 3,
        out_specs=vmem,
        scratch_shapes=[pltpu.VMEM((BLOCK, WIDTH), jnp.bfloat16)] * 4 + [
            pltpu.VMEM((2, BLOCK, WIDTH), jnp.bfloat16),
            pltpu.VMEM((3, BLOCK, WIDTH), jnp.bfloat16),
        ] + [pltpu.VMEM(piece, jnp.bfloat16)] * 11 + [
            pltpu.SemaphoreType.DMA((ROWS, 3, CHUNKS)),
            pltpu.SemaphoreType.DMA((2, 2, CHUNKS)),
            pltpu.SemaphoreType.DMA((2, CHUNKS)),
            pltpu.SemaphoreType.DMA((3,)),
        ],
        compiler_params=pltpu.CompilerParams(
            collective_id=0, has_side_effects=True, vmem_limit_bytes=48 * 1024 * 1024,
        ),
    )(block_list, earlier_span, span_inputs, next_inputs, q_gain, k_gain, out_gain)


def solution(mesh):
    in_specs = (
        P("section", "ctx", None),
        P("section", "ctx", None),
        P("ctx", None),
        P(),
        P("section", None),
        P("section", None),
        P("section", None),
    )
    out_specs = P("section", "ctx", None)
    return jax.shard_map(local, mesh=mesh, in_specs=in_specs, out_specs=out_specs, check_vma=False)
```
